32 devices in a mesh: group: 2 (over y), context: 4 (over z), tensor: 2 (over x), strand: 2 (over core).
Axes of the slice: x: 2, y: 2, z: 4, core: 2. Of those that a mesh axis runs over, the one named last changes fastest.
Arguments:
- trunk_rows: bfloat16 [2, 2048, 1536], P('strand', ('group', 'context'), 'tensor'), parts along dimension 1, may hold values from -6 to 6
- skip_mid: bfloat16 [2, 4096, 1536], P('strand', ('group', 'context'), 'tensor'), parts along dimension 1, may hold values from -6 to 6
- skip_fine: bfloat16 [2, 8192, 1536], P('strand', ('group', 'context'), 'tensor'), parts along dimension 1, may hold values from -6 to 6
- coarse_mid: bfloat16 [1536, 1536], P(None, 'tensor'), may hold values from -0.15625 to 0.15625
- lateral_mid: bfloat16 [1536, 1536], P(None, 'tensor'), may hold values from -0.15625 to 0.15625
- gain_mid: float32 [1536], P('tensor'), may hold values from 0.1 to 1.9
- shift_mid: float32 [1536], P('tensor'), may hold values from -0.5 to 0.5
- depth_mid: bfloat16 [3, 1536], P(None, 'tensor'), may hold values from -3.5 to 3.5
- mixing_mid: bfloat16 [1536, 1536], P(None, 'tensor'), may hold values from -0.15625 to 0.15625
- coarse_fine: bfloat16 [1536, 1536], P(None, 'tensor'), may hold values from -0.15625 to 0.15625
- lateral_fine: bfloat16 [1536, 1536], P(None, 'tensor'), may hold values from -0.15625 to 0.15625
- gain_fine: float32 [1536], P('tensor'), may hold values from 0.1 to 1.9
- shift_fine: float32 [1536], P('tensor'), may hold values from -0.5 to 0.5
- depth_fine: bfloat16 [3, 1536], P(None, 'tensor'), may hold values from -3.5 to 3.5
- mixing_fine: bfloat16 [1536, 1536], P(None, 'tensor'), may hold values from -0.15625 to 0.15625
- head_weight: bfloat16 [1536, 4096], P(None, 'tensor'), may hold values from -0.15625 to 0.15625
Outputs:
- averaged: bfloat16 [2, 8192, 4096], P('strand', ('group', 'context'), 'tensor'), parts along dimension 1
The draws below stay inside these ranges and needn't reach their ends.
There are 2 independent parts, one for each index of `group`. The reference program is written for one: setup_inputs(seed, part) draws one part's arguments, and reference() takes and returns one part's arrays. A program takes and returns all parts, laid end to end along the dimension named above; an argument that names none is the same for every part. Nothing has to cross between parts.
All inputs are finite; a program needn't handle non-finite values.
Results may differ from the reference program's by a relative error of at most 0.0085.
Values may be sent and summed in bfloat16 or wider, within the bound.
A program may use at most 128 MiB of HBM per device.

```python
import jax
import jax.numpy as jnp

C = 1536
TRACKS = 4096
ROWS = 1024
MID = 2048
BINS = 4096


def levels(key, dims, cuts, low, largest):
    level = 1.0
    for dim, blocks in cuts:
        heights = jax.random.uniform(jax.random.fold_in(jax.random.fold_in(key, 6), dim), (blocks,), jnp.float32, low / len(cuts), largest / len(cuts))
        level = level * jnp.repeat(jnp.exp(heights), dims[dim] // blocks).reshape((-1,) + (1,) * (len(dims) - 1 - dim))
    return level


def gaussian(own_key, dims, spread, limit, shards=(), kind=jnp.bfloat16):
    factor_of = levels(own_key, dims, shards, -0.22, 0.18) if shards else 1.0
    entries = jax.random.normal(own_key, dims, jnp.float32) * spread * factor_of
    return jnp.minimum(jnp.maximum(entries, -limit), limit).astype(kind)


def setup_inputs(seed: int = 0, part: int = 0) -> dict:
    streams_of = jax.random.split(jax.random.key(seed), 17)
    own_keys = jax.random.split(jax.random.fold_in(streams_of[16], part), 17)
    trunk_rows = gaussian(own_keys[0], (2, ROWS, C), 1.0, 6.0, ((0, 2), (1, 4), (2, 2)))
    skip_mid = gaussian(own_keys[1], (2, MID, C), 1.0, 6.0, ((0, 2), (1, 4), (2, 2)))
    skip_fine = gaussian(own_keys[2], (2, BINS, C), 1.0, 6.0, ((0, 2), (1, 4), (2, 2)))
    coarse_mid = gaussian(streams_of[3], (C, C), C ** -0.5, 0.15625, ((1, 2),))
    lateral_mid = gaussian(streams_of[4], (C, C), C ** -0.5, 0.15625, ((1, 2),))
    gain_mid = jnp.clip(1.0 + 0.18 * jax.random.normal(streams_of[5], (C,), jnp.float32), 0.1, 1.9)
    shift_mid = jnp.clip(jax.random.uniform(streams_of[6], (C,), jnp.float32, -0.5, 0.5) * levels(streams_of[6], (C,), ((0, 2),), -0.4, 0.0), -0.5, 0.5)
    depth_mid = gaussian(streams_of[7], (3, C), 3 ** -0.5, 3.5, ((1, 2),))
    mixing_mid = gaussian(streams_of[8], (C, C), C ** -0.5, 0.15625, ((1, 2),))
    coarse_fine = gaussian(streams_of[9], (C, C), C ** -0.5, 0.15625, ((1, 2),))
    lateral_fine = gaussian(streams_of[10], (C, C), C ** -0.5, 0.15625, ((1, 2),))
    gain_fine = jnp.clip(1.0 + 0.18 * jax.random.normal(streams_of[11], (C,), jnp.float32), 0.1, 1.9)
    shift_fine = jnp.clip(jax.random.uniform(streams_of[12], (C,), jnp.float32, -0.5, 0.5) * levels(streams_of[12], (C,), ((0, 2),), -0.4, 0.0), -0.5, 0.5)
    depth_fine = gaussian(streams_of[13], (3, C), 3 ** -0.5, 3.5, ((1, 2),))
    mixing_fine = gaussian(streams_of[14], (C, C), C ** -0.5, 0.15625, ((1, 2),))
    head_weight = gaussian(streams_of[15], (C, TRACKS), C ** -0.5, 0.15625, ((1, 2),))
    return dict(trunk_rows=trunk_rows, skip_mid=skip_mid, skip_fine=skip_fine, coarse_mid=coarse_mid, lateral_mid=lateral_mid, gain_mid=gain_mid, shift_mid=shift_mid, depth_mid=depth_mid, mixing_mid=mixing_mid, coarse_fine=coarse_fine, lateral_fine=lateral_fine, gain_fine=gain_fine, shift_fine=shift_fine, depth_fine=depth_fine, mixing_fine=mixing_fine, head_weight=head_weight)


def upsample_section(coarse, lateral_in, coarse_weight, lateral_weight, gain, shift, depth, mixing):
    lifted = jnp.dot(coarse, coarse_weight, preferred_element_type=jnp.float32)
    skipped = jnp.dot(lateral_in, lateral_weight, preferred_element_type=jnp.float32)
    upsampled = jnp.repeat(lifted, 2, axis=0)
    active = jax.nn.gelu(gain * (upsampled + skipped) + shift).astype(jnp.bfloat16)
    padded = jnp.pad(active.astype(jnp.float32), ((1, 1), (0, 0)))
    kernel_taps = depth.astype(jnp.float32)
    depthwise = (kernel_taps[0] * padded[:-2] + kernel_taps[1] * padded[1:-1] + kernel_taps[2] * padded[2:]).astype(jnp.bfloat16)
    return jnp.dot(depthwise, mixing, preferred_element_type=jnp.float32).astype(jnp.bfloat16)


def flip_tracks(values):
    row_count, track_count = values.shape
    swapped = values.reshape(row_count, track_count // 2, 2)[:, :, ::-1].reshape(row_count, track_count)
    track_index = jnp.arange(track_count)
    return jnp.where((track_index < track_count // 2)[None, :], swapped, values)


def reference(trunk_rows, skip_mid, skip_fine, coarse_mid, lateral_mid, gain_mid, shift_mid, depth_mid, mixing_mid, coarse_fine, lateral_fine, gain_fine, shift_fine, depth_fine, mixing_fine, head_weight):
    predictions = []
    for strand in range(2):
        hidden_mid = upsample_section(trunk_rows[strand], skip_mid[strand], coarse_mid, lateral_mid, gain_mid, shift_mid, depth_mid, mixing_mid)
        hidden_fine = upsample_section(hidden_mid, skip_fine[strand], coarse_fine, lateral_fine, gain_fine, shift_fine, depth_fine, mixing_fine)
        logits = jnp.dot(hidden_fine, head_weight, preferred_element_type=jnp.float32)
        predictions.append(jax.nn.softplus(logits).astype(jnp.bfloat16))
    forward = predictions[0].astype(jnp.float32)
    backward = flip_tracks(predictions[1][::-1]).astype(jnp.float32)
    averaged = (0.5 * (forward + backward)).astype(jnp.bfloat16)
    mirrored = flip_tracks(averaged[::-1])
    return jnp.stack([averaged, mirrored])
```

```python
import jax
import jax.numpy as jnp
from jax import lax
from jax.sharding import PartitionSpec as P


def with_halo(block, sides, width):
    for axis, dim in sides:
        count = lax.axis_size(axis)
        forward = [(i, i + 1) for i in range(count - 1)]
        backward = [(target, source) for source, target in forward]
        low = lax.ppermute(
            lax.slice_in_dim(block, block.shape[dim] - width, None, axis=dim), axis, forward
        )
        high = lax.ppermute(lax.slice_in_dim(block, 0, width, axis=dim), axis, backward)
        block = jnp.concatenate([low, block, high], axis=dim)
    return block


def from_partner(value, axis, apart):
    mask = 2**apart
    pairs = [(source, source ^ mask) for source in range(lax.axis_size(axis))]
    return lax.ppermute(value, axis, pairs)


def contract(portion, weight):
    return jnp.dot(portion, weight, preferred_element_type=jnp.float32)


def upsample_section(coarse, lateral_in, coarse_weight, lateral_weight, gain, shift, depth, mixing):
    lifted = contract(lax.all_gather(coarse, "tensor", axis=1, tiled=True), coarse_weight)
    skipped = contract(lax.all_gather(lateral_in, "tensor", axis=1, tiled=True), lateral_weight)
    upsampled = jnp.repeat(lifted, 2, axis=0)
    active = jax.nn.gelu(gain * (upsampled + skipped) + shift).astype(jnp.bfloat16)
    padded = with_halo(active, (("context", 0),), 1).astype(jnp.float32)
    kernel_taps = depth.astype(jnp.float32)
    depthwise = (
        kernel_taps[0] * padded[:-2] + kernel_taps[1] * padded[1:-1] + kernel_taps[2] * padded[2:]
    ).astype(jnp.bfloat16)
    mixed_out = contract(lax.all_gather(depthwise, "tensor", axis=1, tiled=True), mixing)
    return mixed_out.astype(jnp.bfloat16)


def flip_weight(weight, total_tracks):
    depth, track_count = weight.shape
    tile = 128
    row = lax.broadcasted_iota(jnp.int32, (tile, tile), 0)
    column = lax.broadcasted_iota(jnp.int32, (tile, tile), 1)
    swap = (row == (column ^ 1)).astype(weight.dtype)
    swapped = jnp.einsum(
        "kbi,ij->kbj",
        weight.reshape(depth, track_count // tile, tile),
        swap,
        preferred_element_type=weight.dtype,
    ).reshape(depth, track_count)
    track_index = lax.axis_index("tensor") * track_count + jnp.arange(track_count)
    return jnp.where((track_index < total_tracks // 2)[None, :], swapped, weight)


def on_device(
    trunk_rows,
    skip_mid,
    skip_fine,
    coarse_mid,
    lateral_mid,
    gain_mid,
    shift_mid,
    depth_mid,
    mixing_mid,
    coarse_fine,
    lateral_fine,
    gain_fine,
    shift_fine,
    depth_fine,
    mixing_fine,
    head_weight,
):
    hidden_mid = upsample_section(
        trunk_rows[0],
        skip_mid[0],
        coarse_mid,
        lateral_mid,
        gain_mid,
        shift_mid,
        depth_mid,
        mixing_mid,
    )
    hidden_fine = upsample_section(
        hidden_mid,
        skip_fine[0],
        coarse_fine,
        lateral_fine,
        gain_fine,
        shift_fine,
        depth_fine,
        mixing_fine,
    )
    total_tracks = head_weight.shape[1] * lax.axis_size("tensor")
    row_count, width = hidden_fine.shape
    slabs, strands = lax.axis_size("context"), lax.axis_size("strand")
    count = slabs * strands
    crossed = lax.ppermute(
        hidden_fine, ("context", "strand"), [(i, count - 1 - i) for i in range(count)]
    )
    own_logits = contract(lax.all_gather(hidden_fine, "tensor", axis=1, tiled=True), head_weight)
    predicted = jax.nn.softplus(own_logits).astype(jnp.bfloat16)
    reverse = jnp.eye(256, dtype=jnp.bfloat16)[::-1]
    blocks = crossed.reshape(row_count // 256, 256, width)[::-1]
    partner = jnp.einsum(
        "ij,bjk->bik", reverse, blocks, preferred_element_type=jnp.bfloat16
    ).reshape(row_count, width)
    flipped_head = flip_weight(head_weight, total_tracks)
    partner_logits = contract(
        lax.all_gather(partner, "tensor", axis=1, tiled=True), flipped_head
    )
    mirrored = jax.nn.softplus(partner_logits).astype(jnp.bfloat16)
    averaged = (0.5 * (predicted.astype(jnp.float32) + mirrored.astype(jnp.float32))).astype(
        jnp.bfloat16
    )
    return averaged[None]


def solution(mesh):
    in_specs = (
        P("strand", ("group", "context"), "tensor"),
        P("strand", ("group", "context"), "tensor"),
        P("strand", ("group", "context"), "tensor"),
        P(None, "tensor"),
        P(None, "tensor"),
        P("tensor"),
        P("tensor"),
        P(None, "tensor"),
        P(None, "tensor"),
        P(None, "tensor"),
        P(None, "tensor"),
        P("tensor"),
        P("tensor"),
        P(None, "tensor"),
        P(None, "tensor"),
        P(None, "tensor"),
    )
    out_specs = P("strand", ("group", "context"), "tensor")
    return jax.shard_map(
        on_device, mesh=mesh, in_specs=in_specs, out_specs=out_specs, check_vma=False
    )
```

```python
import jax
import jax.numpy as jnp
from jax import lax
from jax.experimental import pallas as pl
from jax.experimental.pallas import tpu as pltpu
from jax.sharding import PartitionSpec as P

MESH = pl.DeviceIdType.MESH
EDGE = 16


def dot(left, right):
    return jnp.dot(left, right, preferred_element_type=jnp.float32)


def gelu(x):
    return 0.5 * x * (1.0 + jnp.tanh(0.7978845608028654 * (x + 0.044715 * (x * x * x))))


def mean_softplus(a, b):
    ea = jnp.exp(-jnp.abs(a))
    eb = jnp.exp(-jnp.abs(b))
    u = ea + eb + ea * eb
    log = jnp.where(u < 1e-3, u * (1.0 - 0.5 * u), jnp.log(1.0 + u))
    return 0.5 * (jnp.maximum(a, 0.0) + jnp.maximum(b, 0.0) + log)


class Gather:
    def __init__(self, peers, buffer, tile, send, recv):
        self.me, self.count = peers
        self.buffer, self.tile, self.send_sem, self.recv_sem = buffer, tile, send, recv
        self.tiles = buffer.shape[1] // tile

    def rows(self, i):
        return pl.ds(pl.multiple_of(i * self.tile, EDGE), self.tile)

    def copy(self, d, slot, i, source=None):
        target = self.buffer.at[slot, self.rows(i)]
        return pltpu.make_async_remote_copy(
            src_ref=target if source is None else source.at[0, self.rows(i)],
            dst_ref=target,
            send_sem=self.send_sem.at[d - 1, i],
            recv_sem=self.recv_sem.at[d - 1, i],
            device_id={"tensor": lax.rem(self.me + d, self.count)},
            device_id_type=MESH,
        )

    def start(self, i, source=None):
        for d in range(1, self.count):
            self.copy(d, self.me, i, source).start()

    def arrived(self, i):
        for d in range(1, self.count):
            self.copy(d, lax.rem(self.me + self.count - d, self.count), i).wait_recv()

    def sent(self):
        @pl.loop(0, self.tiles)
        def _(i):
            for d in range(1, self.count):
                self.copy(d, self.me, i).wait_send()


def kernel(
    sizes,
    trunk, skip_mid, skip_fine,
    coarse_mid, lateral_mid, mixing_mid, coarse_fine, lateral_fine, mixing_fine, head,
    gain_mid, shift_mid, depth_mid, gain_fine, shift_fine, depth_fine,
    out,
    trunk_all, skip_mid_all, skip_fine_all, taps_mid_all, hidden_mid_all, taps_fine_all, own_all,
    partner_all,
    active_mid, active_fine,
    w_coarse_mid, w_lateral_mid, w_mixing_mid, w_coarse_fine, w_lateral_fine, w_mixing_fine,
    w_head, w_flipped,
    expanded, turned, result, doubler, reverser, swapper,
    local_sem, out_sem,
    s0, r0, s1, r1, s2, r2, s3, r3, s4, r4, s5, r5, s6, r6, s7, r7,
    mirror_send, mirror_recv, edge_send, edge_recv,
):
    tensors, contexts, tile_mid, tile_fine = sizes
    me = lax.axis_index("tensor")
    slab = lax.axis_index("context")
    strand = lax.axis_index("strand")
    after = {"context": lax.rem(slab + 1, contexts)}
    before = {"context": lax.rem(slab + contexts - 1, contexts)}
    mirror = {"context": contexts - 1 - slab, "strand": 1 - strand}
    width = active_mid.shape[1]
    tracks = w_head.shape[1]
    step = 256 if width % 256 == 0 else width
    peers = (me, tensors)

    locals_ = []
    for source, target in (
        (trunk.at[0], trunk_all.at[me]),
        (skip_mid.at[0], skip_mid_all.at[me]),
        (head, w_head),
        (coarse_mid, w_coarse_mid),
        (lateral_mid, w_lateral_mid),
        (mixing_mid, w_mixing_mid),
        (skip_fine.at[0], skip_fine_all.at[me]),
        (coarse_fine, w_coarse_fine),
        (lateral_fine, w_lateral_fine),
        (mixing_fine, w_mixing_fine),
    ):
        copy = pltpu.make_async_copy(source, target, local_sem.at[len(locals_)])
        copy.start()
        locals_.append(copy)

    barrier = pltpu.get_barrier_semaphore()
    for d in range(1, tensors):
        pl.semaphore_signal(
            barrier, inc=1, device_id={"tensor": lax.rem(me + d, tensors)}, device_id_type=MESH
        )
    for target in (after, before, mirror):
        pl.semaphore_signal(barrier, inc=1, device_id=target, device_id_type=MESH)
    pl.semaphore_wait(barrier, tensors + 2)

    g_trunk = Gather(peers, trunk_all, trunk_all.shape[1], s0, r0)
    g_skip_mid = Gather(peers, skip_mid_all, skip_mid_all.shape[1], s1, r1)
    g_skip_fine = Gather(peers, skip_fine_all, tile_fine, s2, r2)
    g_taps_mid = Gather(peers, taps_mid_all, tile_mid, s3, r3)
    g_hidden_mid = Gather(peers, hidden_mid_all, tile_mid, s4, r4)
    g_taps_fine = Gather(peers, taps_fine_all, tile_fine, s5, r5)
    g_own = Gather(peers, own_all, tile_fine, s6, r6)
    g_partner = Gather(peers, partner_all, tile_fine, s7, r7)
    fine_tiles = g_own.tiles

    g_trunk.start(0, trunk)
    g_skip_mid.start(0, skip_mid)

    def iotas(shape):
        return (
            lax.broadcasted_iota(jnp.int32, shape, 0),
            lax.broadcasted_iota(jnp.int32, shape, 1),
        )

    row, column = iotas(doubler.shape)
    doubler[...] = jnp.where(
        (row == 2 * column) | (row == 2 * column + 1), 1.0, 0.0
    ).astype(jnp.bfloat16)
    row, column = iotas(reverser.shape)
    reverser[...] = jnp.where(row + column == tile_fine - 1, 1.0, 0.0).astype(jnp.bfloat16)
    row, column = iotas(swapper.shape)
    neighbour = jnp.where(lax.rem(column, 2) == 0, column + 1, column - 1)

    locals_[2].wait()

    @pl.loop(0, tracks // 256)
    def _(n):
        columns = pl.ds(pl.multiple_of(n * 256, 256), 256)
        first = me * tracks + n * 256
        flips = first < (tracks * tensors) // 2
        swapper[...] = jnp.where(
            row == jnp.where(flips, neighbour, column), 1.0, 0.0
        ).astype(jnp.bfloat16)
        for j in range(tensors):
            depth = pl.ds(j * width, width)
            w_flipped[depth, columns] = dot(w_head[depth, columns], swapper[...]).astype(
                jnp.bfloat16
            )

    def project(i, tile, coarse, lateral, w_coarse, w_lateral, gain, shift, active):
        half = pl.ds(pl.multiple_of(i * (tile // 2), EDGE), tile // 2)
        rows = pl.ds(pl.multiple_of(i * tile, EDGE), tile)
        for j in range(tensors):
            expanded[j, :tile] = dot(doubler[:tile, : tile // 2], coarse[j, half]).astype(
                jnp.bfloat16
            )

        @pl.loop(0, width // step)
        def _(n):
            columns = pl.ds(pl.multiple_of(n * step, 128), step)
            total = jnp.zeros((tile, step), jnp.float32)
            for j in range(tensors):
                depth = pl.ds(j * width, width)
                total += dot(expanded[j, :tile], w_coarse[depth, columns])
                total += dot(lateral[j, rows], w_lateral[depth, columns])
            value = gelu(gain[:, columns] * total + shift[:, columns])
            active[pl.ds(pl.multiple_of(EDGE + i * tile, EDGE), tile), columns] = value.astype(
                jnp.bfloat16
            )

    def edges(active, k):
        length = active.shape[0] - 2 * EDGE
        up = pltpu.make_async_remote_copy(
            src_ref=active.at[pl.ds(length, EDGE)],
            dst_ref=active.at[pl.ds(0, EDGE)],
            send_sem=edge_send.at[k],
            recv_sem=edge_recv.at[k],
            device_id=after,
            device_id_type=MESH,
        )
        down = pltpu.make_async_remote_copy(
            src_ref=active.at[pl.ds(EDGE, EDGE)],
            dst_ref=active.at[pl.ds(length + EDGE, EDGE)],
            send_sem=edge_send.at[k + 1],
            recv_sem=edge_recv.at[k + 1],
            device_id=before,
            device_id_type=MESH,
        )
        return up, down

    def depthwise(i, tile, tiles, active, taps, target):
        start = pl.multiple_of(i * tile, EDGE)

        @pl.loop(0, width // step)
        def _(n):
            columns = pl.ds(pl.multiple_of(n * step, 128), step)
            middle = active[pl.ds(pl.multiple_of(start + EDGE, EDGE), tile), columns].astype(
                jnp.float32
            )
            low = active[pl.ds(start, EDGE), columns].astype(jnp.float32)[EDGE - 1 :]
            high = active[
                pl.ds(pl.multiple_of(start + EDGE + tile, EDGE), EDGE), columns
            ].astype(jnp.float32)[:1]
            low = jnp.where((i == 0) & (slab == 0), 0.0, low)
            high = jnp.where((i == tiles - 1) & (slab == contexts - 1), 0.0, high)
            place = lax.broadcasted_iota(jnp.int32, middle.shape, 0)
            previous = jnp.where(place == 0, low, pltpu.roll(middle, 1, 0))
            following = jnp.where(place == tile - 1, high, pltpu.roll(middle, tile - 1, 0))
            tap = taps[:, columns].astype(jnp.float32)
            value = tap[0:1] * previous + tap[1:2] * middle + tap[2:3] * following
            target[me, pl.ds(start, tile), columns] = value.astype(jnp.bfloat16)

    def mix(i, tile, source, weight, target):
        rows = pl.ds(pl.multiple_of(i * tile, EDGE), tile)

        @pl.loop(0, width // step)
        def _(n):
            columns = pl.ds(pl.multiple_of(n * step, 128), step)
            total = jnp.zeros((tile, step), jnp.float32)
            for j in range(tensors):
                total += dot(source[j, rows], weight[pl.ds(j * width, width), columns])
            target[me, rows, columns] = total.astype(jnp.bfloat16)

    for k in (0, 1, 3, 4, 5):
        locals_[k].wait()
    g_trunk.arrived(0)
    g_skip_mid.arrived(0)
    g_skip_fine.start(0, skip_fine)

    @pl.loop(0, g_taps_mid.tiles)
    def _(i):
        project(
            i, tile_mid, trunk_all, skip_mid_all, w_coarse_mid, w_lateral_mid,
            gain_mid, shift_mid, active_mid,
        )

    edges_mid = edges(active_mid, 0)
    for copy in edges_mid:
        copy.start()
    for copy in edges_mid:
        copy.wait()

    @pl.loop(0, g_taps_mid.tiles)
    def _(i):
        depthwise(i, tile_mid, g_taps_mid.tiles, active_mid, depth_mid, taps_mid_all)
        g_taps_mid.start(i)

    cut = min(2, fine_tiles)
    for k in range(1, cut):
        g_skip_fine.start(k, skip_fine)

    @pl.loop(0, g_taps_mid.tiles)
    def _(i):
        g_taps_mid.arrived(i)
        mix(i, tile_mid, taps_mid_all, w_mixing_mid, hidden_mid_all)
        g_hidden_mid.start(i)

    for k in range(cut, fine_tiles):
        g_skip_fine.start(k, skip_fine)

    for k in (6, 7, 8, 9):
        locals_[k].wait()

    @pl.loop(0, g_hidden_mid.tiles)
    def _(i):
        g_hidden_mid.arrived(i)

    @pl.loop(0, fine_tiles)
    def _(i):
        g_skip_fine.arrived(i)
        project(
            i, tile_fine, hidden_mid_all, skip_fine_all, w_coarse_fine, w_lateral_fine,
            gain_fine, shift_fine, active_fine,
        )

    edges_fine = edges(active_fine, 2)
    for copy in edges_fine:
        copy.start()
    for copy in edges_fine:
        copy.wait()

    @pl.loop(0, fine_tiles)
    def _(i):
        depthwise(i, tile_fine, fine_tiles, active_fine, depth_fine, taps_fine_all)
        g_taps_fine.start(i)

    def cross(i):
        return pltpu.make_async_remote_copy(
            src_ref=own_all.at[me, g_own.rows(i)],
            dst_ref=partner_all.at[me, g_own.rows(i)],
            send_sem=mirror_send.at[i],
            recv_sem=mirror_recv.at[i],
            device_id=mirror,
            device_id_type=MESH,
        )

    @pl.loop(0, fine_tiles)
    def _(i):
        g_taps_fine.arrived(i)
        mix(i, tile_fine, taps_fine_all, w_mixing_fine, own_all)
        cross(i).start()
        g_own.start(i)

    @pl.loop(0, fine_tiles)
    def _(i):
        g_own.arrived(i)

    def write(k):
        rows = g_own.rows(k)
        return pltpu.make_async_copy(result.at[rows], out.at[0, rows], out_sem.at[k])

    def predict(k):
        rows = g_own.rows(fine_tiles - 1 - k)
        g_partner.arrived(k)
        for j in range(tensors):
            turned[j] = dot(reverser[...], partner_all[j, g_own.rows(k)]).astype(jnp.bfloat16)

        @pl.loop(0, tracks // 256)
        def _(n):
            columns = pl.ds(pl.multiple_of(n * 256, 256), 256)
            a = jnp.zeros((tile_fine, 256), jnp.float32)
            b = jnp.zeros((tile_fine, 256), jnp.float32)
            for j in range(tensors):
                depth = pl.ds(j * width, width)
                a += dot(own_all[j, rows], w_head[depth, columns])
                b += dot(turned[j], w_flipped[depth, columns])
            result[rows, columns] = mean_softplus(a, b).astype(jnp.bfloat16)

        write(fine_tiles - 1 - k).start()

    @pl.loop(0, fine_tiles + 1)
    def _(k):
        @pl.when(k < fine_tiles)
        def _():
            cross(k).wait_recv()
            g_partner.start(k)

        @pl.when(k > 0)
        def _():
            predict(k - 1)

    for gather in (
        g_trunk, g_skip_mid, g_skip_fine, g_taps_mid, g_hidden_mid, g_taps_fine, g_own, g_partner
    ):
        gather.sent()

    @pl.loop(0, fine_tiles)
    def _(i):
        cross(i).wait_send()
        write(i).wait()


def solution(mesh):
    tensors, contexts = mesh.shape["tensor"], mesh.shape["context"]

    def on_device(
        trunk_rows, skip_mid, skip_fine, coarse_mid, lateral_mid, gain_mid, shift_mid, depth_mid,
        mixing_mid, coarse_fine, lateral_fine, gain_fine, shift_fine, depth_fine, mixing_fine,
        head_weight,
    ):
        _, coarse_rows, width = trunk_rows.shape
        mid_rows, fine_rows = skip_mid.shape[1], skip_fine.shape[1]
        depth, tracks = head_weight.shape
        tile_mid, tile_fine = min(128, mid_rows), min(256, fine_rows)
        mid_tiles, fine_tiles = mid_rows // tile_mid, fine_rows // tile_fine
        peers = max(tensors - 1, 1)
        bf16 = jnp.bfloat16

        def everyone(rows):
            return pltpu.VMEM((tensors, rows, width), bf16)

        square = pltpu.VMEM((depth, width), bf16)
        semaphores = []
        for tiles in (
            1, 1, fine_tiles, mid_tiles, mid_tiles, fine_tiles, fine_tiles, fine_tiles
        ):
            semaphores += [pltpu.SemaphoreType.DMA((peers, tiles))] * 2
        anywhere = pl.BlockSpec(memory_space=pl.ANY)
        inside = pl.BlockSpec(memory_space=pltpu.VMEM)

        def body(*refs):
            kernel((tensors, contexts, tile_mid, tile_fine), *refs)

        macs = width * depth * (coarse_rows + 2 * mid_rows + mid_rows + 2 * fine_rows)
        macs += 2 * fine_rows * depth * tracks
        return pl.pallas_call(
            body,
            out_shape=jax.ShapeDtypeStruct((1, fine_rows, tracks), bf16),
            in_specs=[anywhere] * 10 + [inside] * 6,
            out_specs=anywhere,
            scratch_shapes=[
                everyone(coarse_rows),
                everyone(mid_rows),
                everyone(fine_rows),
                everyone(mid_rows),
                everyone(mid_rows),
                everyone(fine_rows),
                everyone(fine_rows),
                everyone(fine_rows),
                pltpu.VMEM((mid_rows + 2 * EDGE, width), bf16),
                pltpu.VMEM((fine_rows + 2 * EDGE, width), bf16),
                square, square, square, square, square, square,
                pltpu.VMEM((depth, tracks), bf16),
                pltpu.VMEM((depth, tracks), bf16),
                everyone(tile_fine),
                everyone(tile_fine),
                pltpu.VMEM((fine_rows, tracks), bf16),
                pltpu.VMEM((tile_fine, tile_fine // 2), bf16),
                pltpu.VMEM((tile_fine, tile_fine), bf16),
                pltpu.VMEM((256, 256), bf16),
                pltpu.SemaphoreType.DMA((10,)),
                pltpu.SemaphoreType.DMA((fine_tiles,)),
                *semaphores,
                pltpu.SemaphoreType.DMA((fine_tiles,)),
                pltpu.SemaphoreType.DMA((fine_tiles,)),
                pltpu.SemaphoreType.DMA((4,)),
                pltpu.SemaphoreType.DMA((4,)),
            ],
            compiler_params=pltpu.CompilerParams(
                collective_id=0, has_side_effects=True, vmem_limit_bytes=60 * 2**20
            ),
            cost_estimate=pl.CostEstimate(
                flops=2 * macs, bytes_accessed=32 * 2**20, transcendentals=6 * 2**20
            ),
            name="upsample_and_predict",
        )(
            trunk_rows, skip_mid, skip_fine, coarse_mid, lateral_mid, mixing_mid, coarse_fine,
            lateral_fine, mixing_fine, head_weight, gain_mid[None], shift_mid[None], depth_mid,
            gain_fine[None], shift_fine[None], depth_fine,
        )

    rows = P("strand", ("group", "context"), "tensor")
    weight, vector = P(None, "tensor"), P("tensor")
    section = (weight, weight, vector, vector, weight, weight)
    return jax.shard_map(
        on_device,
        mesh=mesh,
        in_specs=(rows, rows, rows, *section, *section, weight),
        out_specs=rows,
        check_vma=False,
    )
```

```python
import jax
import jax.numpy as jnp
from jax import lax
from jax.experimental import pallas as pl
from jax.experimental.pallas import tpu as pltpu
from jax.sharding import PartitionSpec as P

MESH = pl.DeviceIdType.MESH
EDGE = 16


def dot(left, right):
    return jnp.dot(left, right, preferred_element_type=jnp.float32)


def gelu(x):
    return 0.5 * x * (1.0 + jnp.tanh(0.7978845608028654 * (x + 0.044715 * (x * x * x))))


def mean_softplus(a, b):
    ea = jnp.exp(-jnp.abs(a))
    eb = jnp.exp(-jnp.abs(b))
    u = ea + eb + ea * eb
    log = jnp.where(u < 1e-3, u * (1.0 - 0.5 * u), jnp.log(1.0 + u))
    return 0.5 * (jnp.maximum(a, 0.0) + jnp.maximum(b, 0.0) + log)


class Gather:
    def __init__(self, peers, buffer, tile, send, recv):
        self.me, self.count = peers
        self.buffer, self.tile, self.send_sem, self.recv_sem = buffer, tile, send, recv
        self.tiles = buffer.shape[1] // tile

    def rows(self, i):
        return pl.ds(pl.multiple_of(i * self.tile, EDGE), self.tile)

    def copy(self, d, slot, i, source=None):
        target = self.buffer.at[slot, self.rows(i)]
        return pltpu.make_async_remote_copy(
            src_ref=target if source is None else source.at[0, self.rows(i)],
            dst_ref=target,
            send_sem=self.send_sem.at[d - 1, i],
            recv_sem=self.recv_sem.at[d - 1, i],
            device_id={"tensor": lax.rem(self.me + d, self.count)},
            device_id_type=MESH,
        )

    def start(self, i, source=None):
        for d in range(1, self.count):
            self.copy(d, self.me, i, source).start()

    def arrived(self, i):
        for d in range(1, self.count):
            self.copy(d, lax.rem(self.me + self.count - d, self.count), i).wait_recv()

    def sent(self):
        @pl.loop(0, self.tiles)
        def _(i):
            for d in range(1, self.count):
                self.copy(d, self.me, i).wait_send()


def kernel(
    sizes,
    trunk, skip_mid, skip_fine,
    coarse_mid, lateral_mid, mixing_mid, coarse_fine, lateral_fine, mixing_fine, head,
    gain_mid, shift_mid, depth_mid, gain_fine, shift_fine, depth_fine,
    out,
    trunk_all, skip_mid_all, skip_fine_all, taps_mid_all, hidden_mid_all, taps_fine_all, own_all,
    partner_all,
    active_mid, active_fine,
    w_coarse_mid, w_lateral_mid, w_mixing_mid, w_coarse_fine, w_lateral_fine, w_mixing_fine,
    w_head, w_flipped,
    vectors, expanded, turned, result, doubler, reverser, swapper,
    local_sem, out_sem,
    s0, r0, s1, r1, s2, r2, s3, r3, s4, r4, s5, r5, s6, r6, s7, r7,
    mirror_send, mirror_recv, edge_send, edge_recv,
):
    tensors, contexts, tile_mid, tile_fine = sizes
    me = lax.axis_index("tensor")
    slab = lax.axis_index("context")
    strand = lax.axis_index("strand")
    after = {"context": lax.rem(slab + 1, contexts)}
    before = {"context": lax.rem(slab + contexts - 1, contexts)}
    mirror = {"context": contexts - 1 - slab, "strand": 1 - strand}
    width = active_mid.shape[1]
    tracks = w_head.shape[1]
    step = 256 if width % 256 == 0 else width
    peers = (me, tensors)

    locals_ = []
    for source, target in (
        (trunk.at[0], trunk_all.at[me]),
        (skip_mid.at[0], skip_mid_all.at[me]),
        (head, w_head),
        (coarse_mid, w_coarse_mid),
        (lateral_mid, w_lateral_mid),
        (mixing_mid, w_mixing_mid),
        (skip_fine.at[0], skip_fine_all.at[me]),
        (coarse_fine, w_coarse_fine),
        (lateral_fine, w_lateral_fine),
        (mixing_fine, w_mixing_fine),
    ):
        copy = pltpu.make_async_copy(source, target, local_sem.at[len(locals_)])
        copy.start()
        locals_.append(copy)

    barrier = pltpu.get_barrier_semaphore()
    for d in range(1, tensors):
        pl.semaphore_signal(
            barrier, inc=1, device_id={"tensor": lax.rem(me + d, tensors)}, device_id_type=MESH
        )
    for target in (after, before, mirror):
        pl.semaphore_signal(barrier, inc=1, device_id=target, device_id_type=MESH)
    pl.semaphore_wait(barrier, tensors + 2)

    g_trunk = Gather(peers, trunk_all, tile_mid // 2, s0, r0)
    g_skip_mid = Gather(peers, skip_mid_all, tile_mid, s1, r1)
    g_skip_fine = Gather(peers, skip_fine_all, tile_fine, s2, r2)
    g_taps_mid = Gather(peers, taps_mid_all, tile_mid, s3, r3)
    g_hidden_mid = Gather(peers, hidden_mid_all, tile_mid, s4, r4)
    g_taps_fine = Gather(peers, taps_fine_all, tile_fine, s5, r5)
    g_own = Gather(peers, own_all, tile_fine, s6, r6)
    g_partner = Gather(peers, partner_all, tile_fine, s7, r7)
    fine_tiles = g_own.tiles

    for k in range(g_trunk.tiles):
        g_trunk.start(k, trunk)
        g_skip_mid.start(k, skip_mid)
    g_skip_fine.start(0, skip_fine)
    for k, vector in enumerate((gain_mid, shift_mid, gain_fine, shift_fine)):
        vectors[k : k + 1] = vector[...].reshape(1, width)

    def iotas(shape):
        return (
            lax.broadcasted_iota(jnp.int32, shape, 0),
            lax.broadcasted_iota(jnp.int32, shape, 1),
        )

    row, column = iotas(doubler.shape)
    doubler[...] = jnp.where(
        (row == 2 * column) | (row == 2 * column + 1), 1.0, 0.0
    ).astype(jnp.bfloat16)
    row, column = iotas(reverser.shape)
    reverser[...] = jnp.where(row + column == tile_fine - 1, 1.0, 0.0).astype(jnp.bfloat16)
    row, column = iotas(swapper.shape)
    neighbour = jnp.where(lax.rem(column, 2) == 0, column + 1, column - 1)

    locals_[2].wait()

    @pl.loop(0, tracks // 256)
    def _(n):
        columns = pl.ds(pl.multiple_of(n * 256, 256), 256)
        first = me * tracks + n * 256
        flips = first < (tracks * tensors) // 2
        swapper[...] = jnp.where(
            row == jnp.where(flips, neighbour, column), 1.0, 0.0
        ).astype(jnp.bfloat16)
        for j in range(tensors):
            depth = pl.ds(j * width, width)
            w_flipped[depth, columns] = dot(w_head[depth, columns], swapper[...]).astype(
                jnp.bfloat16
            )

    def project(i, tile, coarse, lateral, w_coarse, w_lateral, k, active):
        half = pl.ds(pl.multiple_of(i * (tile // 2), EDGE), tile // 2)
        rows = pl.ds(pl.multiple_of(i * tile, EDGE), tile)
        for j in range(tensors):
            expanded[j, :tile] = dot(doubler[:tile, : tile // 2], coarse[j, half]).astype(
                jnp.bfloat16
            )

        @pl.loop(0, width // step)
        def _(n):
            columns = pl.ds(pl.multiple_of(n * step, 128), step)
            total = jnp.zeros((tile, step), jnp.float32)
            for j in range(tensors):
                depth = pl.ds(j * width, width)
                total += dot(expanded[j, :tile], w_coarse[depth, columns])
                total += dot(lateral[j, rows], w_lateral[depth, columns])
            value = gelu(vectors[k : k + 1, columns] * total + vectors[k + 1 : k + 2, columns])
            active[pl.ds(pl.multiple_of(EDGE + i * tile, EDGE), tile), columns] = value.astype(
                jnp.bfloat16
            )

    def edges(active, k):
        length = active.shape[0] - 2 * EDGE
        up = pltpu.make_async_remote_copy(
            src_ref=active.at[pl.ds(length, EDGE)],
            dst_ref=active.at[pl.ds(0, EDGE)],
            send_sem=edge_send.at[k],
            recv_sem=edge_recv.at[k],
            device_id=after,
            device_id_type=MESH,
        )
        down = pltpu.make_async_remote_copy(
            src_ref=active.at[pl.ds(EDGE, EDGE)],
            dst_ref=active.at[pl.ds(length + EDGE, EDGE)],
            send_sem=edge_send.at[k + 1],
            recv_sem=edge_recv.at[k + 1],
            device_id=before,
            device_id_type=MESH,
        )
        return up, down

    def depthwise(i, tile, tiles, active, taps, target):
        start = pl.multiple_of(i * tile, EDGE)

        @pl.loop(0, width // step)
        def _(n):
            columns = pl.ds(pl.multiple_of(n * step, 128), step)
            middle = active[pl.ds(pl.multiple_of(start + EDGE, EDGE), tile), columns].astype(
                jnp.float32
            )
            low = active[pl.ds(start, EDGE), columns].astype(jnp.float32)[EDGE - 1 :]
            high = active[
                pl.ds(pl.multiple_of(start + EDGE + tile, EDGE), EDGE), columns
            ].astype(jnp.float32)[:1]
            low = jnp.where((i == 0) & (slab == 0), 0.0, low)
            high = jnp.where((i == tiles - 1) & (slab == contexts - 1), 0.0, high)
            place = lax.broadcasted_iota(jnp.int32, middle.shape, 0)
            previous = jnp.where(place == 0, low, pltpu.roll(middle, 1, 0))
            following = jnp.where(place == tile - 1, high, pltpu.roll(middle, tile - 1, 0))
            tap = taps[:, columns].astype(jnp.float32)
            value = tap[0:1] * previous + tap[1:2] * middle + tap[2:3] * following
            target[me, pl.ds(start, tile), columns] = value.astype(jnp.bfloat16)

    def mix(i, tile, source, weight, target):
        rows = pl.ds(pl.multiple_of(i * tile, EDGE), tile)

        @pl.loop(0, width // step)
        def _(n):
            columns = pl.ds(pl.multiple_of(n * step, 128), step)
            total = jnp.zeros((tile, step), jnp.float32)
            for j in range(tensors):
                total += dot(source[j, rows], weight[pl.ds(j * width, width), columns])
            target[me, rows, columns] = total.astype(jnp.bfloat16)

    for k in (0, 1, 3, 4, 5):
        locals_[k].wait()

    def section(tiles, project_tile, taps_tile, active, k):
        up, down = edges(active, k)
        project_tile(0)
        down.start()
        project_tile(1)

        @pl.loop(1, tiles - 1)
        def _(i):
            project_tile(i + 1)

            @pl.when(i == tiles - 2)
            def _():
                up.start()

            taps_tile(i)

        down.wait_recv()
        taps_tile(tiles - 1)
        up.wait_recv()
        taps_tile(0)
        up.wait_send()
        down.wait_send()

    def project_mid(i):
        g_trunk.arrived(i)
        g_skip_mid.arrived(i)
        project(
            i, tile_mid, trunk_all, skip_mid_all, w_coarse_mid, w_lateral_mid, 0, active_mid
        )

    def taps_mid(i):
        depthwise(i, tile_mid, g_taps_mid.tiles, active_mid, depth_mid, taps_mid_all)
        g_taps_mid.start(i)

    section(g_taps_mid.tiles, project_mid, taps_mid, active_mid, 0)

    cut = min(2, fine_tiles)
    for k in range(1, cut):
        g_skip_fine.start(k, skip_fine)

    @pl.loop(0, g_taps_mid.tiles)
    def _(n):
        i = lax.rem(n + 1, g_taps_mid.tiles)
        g_taps_mid.arrived(i)
        mix(i, tile_mid, taps_mid_all, w_mixing_mid, hidden_mid_all)
        g_hidden_mid.start(i)

    for k in range(cut, fine_tiles):
        g_skip_fine.start(k, skip_fine)

    for k in (6, 7, 8, 9):
        locals_[k].wait()

    @pl.loop(0, g_hidden_mid.tiles)
    def _(i):
        g_hidden_mid.arrived(i)

    def project_fine(i):
        g_skip_fine.arrived(i)
        project(
            i, tile_fine, hidden_mid_all, skip_fine_all, w_coarse_fine, w_lateral_fine, 2,
            active_fine,
        )

    def taps_fine(i):
        depthwise(i, tile_fine, fine_tiles, active_fine, depth_fine, taps_fine_all)
        g_taps_fine.start(i)

    section(fine_tiles, project_fine, taps_fine, active_fine, 2)

    def cross(i):
        return pltpu.make_async_remote_copy(
            src_ref=own_all.at[me, g_own.rows(i)],
            dst_ref=partner_all.at[me, g_own.rows(i)],
            send_sem=mirror_send.at[i],
            recv_sem=mirror_recv.at[i],
            device_id=mirror,
            device_id_type=MESH,
        )

    @pl.loop(0, fine_tiles)
    def _(n):
        i = lax.rem(n + 1, fine_tiles)
        g_taps_fine.arrived(i)
        mix(i, tile_fine, taps_fine_all, w_mixing_fine, own_all)
        cross(i).start()
        g_own.start(i)

    @pl.loop(0, fine_tiles)
    def _(i):
        g_own.arrived(i)

    def write(k):
        rows = g_own.rows(k)
        return pltpu.make_async_copy(result.at[rows], out.at[0, rows], out_sem.at[k])

    def predict(k):
        rows = g_own.rows(fine_tiles - 1 - k)
        g_partner.arrived(k)
        for j in range(tensors):
            turned[j] = dot(reverser[...], partner_all[j, g_own.rows(k)]).astype(jnp.bfloat16)

        @pl.loop(0, tracks // 256)
        def _(n):
            columns = pl.ds(pl.multiple_of(n * 256, 256), 256)
            a = jnp.zeros((tile_fine, 256), jnp.float32)
            b = jnp.zeros((tile_fine, 256), jnp.float32)
            for j in range(tensors):
                depth = pl.ds(j * width, width)
                a += dot(own_all[j, rows], w_head[depth, columns])
                b += dot(turned[j], w_flipped[depth, columns])
            result[rows, columns] = mean_softplus(a, b).astype(jnp.bfloat16)

        write(fine_tiles - 1 - k).start()

    @pl.loop(0, fine_tiles + 1)
    def _(n):
        k = lax.rem(n + 1, fine_tiles)

        @pl.when(n < fine_tiles)
        def _():
            cross(k).wait_recv()
            g_partner.start(k)

        @pl.when(n > 0)
        def _():
            predict(lax.rem(n, fine_tiles))

    for gather in (
        g_trunk, g_skip_mid, g_skip_fine, g_taps_mid, g_hidden_mid, g_taps_fine, g_own, g_partner
    ):
        gather.sent()

    @pl.loop(0, fine_tiles)
    def _(i):
        cross(i).wait_send()
        write(i).wait()


def solution(mesh):
    tensors, contexts = mesh.shape["tensor"], mesh.shape["context"]

    def on_device(
        trunk_rows, skip_mid, skip_fine, coarse_mid, lateral_mid, gain_mid, shift_mid, depth_mid,
        mixing_mid, coarse_fine, lateral_fine, gain_fine, shift_fine, depth_fine, mixing_fine,
        head_weight,
    ):
        _, coarse_rows, width = trunk_rows.shape
        mid_rows, fine_rows = skip_mid.shape[1], skip_fine.shape[1]
        depth, tracks = head_weight.shape
        tile_mid, tile_fine = min(128, mid_rows), min(256, fine_rows)
        mid_tiles, fine_tiles = mid_rows // tile_mid, fine_rows // tile_fine
        peers = max(tensors - 1, 1)
        bf16 = jnp.bfloat16

        def everyone(rows):
            return pltpu.VMEM((tensors, rows, width), bf16)

        square = pltpu.VMEM((depth, width), bf16)
        semaphores = []
        for tiles in (
            mid_tiles, mid_tiles, fine_tiles, mid_tiles, mid_tiles, fine_tiles, fine_tiles, fine_tiles
        ):
            semaphores += [pltpu.SemaphoreType.DMA((peers, tiles))] * 2
        anywhere = pl.BlockSpec(memory_space=pl.ANY)
        inside = pl.BlockSpec(memory_space=pltpu.VMEM)

        def body(*refs):
            kernel((tensors, contexts, tile_mid, tile_fine), *refs)

        macs = width * depth * (coarse_rows + 2 * mid_rows + mid_rows + 2 * fine_rows)
        macs += 2 * fine_rows * depth * tracks
        return pl.pallas_call(
            body,
            out_shape=jax.ShapeDtypeStruct((1, fine_rows, tracks), bf16),
            in_specs=[anywhere] * 10 + [inside] * 6,
            out_specs=anywhere,
            scratch_shapes=[
                everyone(coarse_rows),
                everyone(mid_rows),
                everyone(fine_rows),
                everyone(mid_rows),
                everyone(mid_rows),
                everyone(fine_rows),
                everyone(fine_rows),
                everyone(fine_rows),
                pltpu.VMEM((mid_rows + 2 * EDGE, width), bf16),
                pltpu.VMEM((fine_rows + 2 * EDGE, width), bf16),
                square, square, square, square, square, square,
                pltpu.VMEM((depth, tracks), bf16),
                pltpu.VMEM((depth, tracks), bf16),
                pltpu.VMEM((4, width), jnp.float32),
                everyone(tile_fine),
                everyone(tile_fine),
                pltpu.VMEM((fine_rows, tracks), bf16),
                pltpu.VMEM((tile_fine, tile_fine // 2), bf16),
                pltpu.VMEM((tile_fine, tile_fine), bf16),
                pltpu.VMEM((256, 256), bf16),
                pltpu.SemaphoreType.DMA((10,)),
                pltpu.SemaphoreType.DMA((fine_tiles,)),
                *semaphores,
                pltpu.SemaphoreType.DMA((fine_tiles,)),
                pltpu.SemaphoreType.DMA((fine_tiles,)),
                pltpu.SemaphoreType.DMA((4,)),
                pltpu.SemaphoreType.DMA((4,)),
            ],
            compiler_params=pltpu.CompilerParams(
                collective_id=0, has_side_effects=True, vmem_limit_bytes=60 * 2**20
            ),
            cost_estimate=pl.CostEstimate(
                flops=2 * macs, bytes_accessed=32 * 2**20, transcendentals=6 * 2**20
            ),
            name="upsample_and_predict",
        )(
            trunk_rows, skip_mid, skip_fine, coarse_mid, lateral_mid, mixing_mid, coarse_fine,
            lateral_fine, mixing_fine, head_weight, gain_mid, shift_mid, depth_mid,
            gain_fine, shift_fine, depth_fine,
        )

    rows = P("strand", ("group", "context"), "tensor")
    weight, vector = P(None, "tensor"), P("tensor")
    section = (weight, weight, vector, vector, weight, weight)
    return jax.shard_map(
        on_device,
        mesh=mesh,
        in_specs=(rows, rows, rows, *section, *section, weight),
        out_specs=rows,
        check_vma=False,
    )
```

```python
import jax
import jax.numpy as jnp
from jax import lax
from jax.experimental import pallas as pl
from jax.experimental.pallas import tpu as pltpu
from jax.sharding import PartitionSpec as P

MESH = pl.DeviceIdType.MESH
EDGE = 16


def dot(left, right):
    return jnp.dot(left, right, preferred_element_type=jnp.float32)


def gelu(x):
    return 0.5 * x * (1.0 + jnp.tanh(0.7978845608028654 * (x + 0.044715 * (x * x * x))))


def mean_softplus(a, b):
    ea = jnp.exp(-jnp.abs(a))
    eb = jnp.exp(-jnp.abs(b))
    u = ea + eb + ea * eb
    log = jnp.where(u < 1e-3, u * (1.0 - 0.5 * u), jnp.log(1.0 + u))
    return 0.5 * (jnp.maximum(a, 0.0) + jnp.maximum(b, 0.0) + log)


class Gather:
    def __init__(self, peers, buffer, tile, send, recv):
        self.me, self.count = peers
        self.buffer, self.tile, self.send_sem, self.recv_sem = buffer, tile, send, recv
        self.tiles = buffer.shape[1] // tile

    def rows(self, i):
        return pl.ds(pl.multiple_of(i * self.tile, EDGE), self.tile)

    def copy(self, d, slot, i, source=None):
        target = self.buffer.at[slot, self.rows(i)]
        return pltpu.make_async_remote_copy(
            src_ref=target if source is None else source.at[0, self.rows(i)],
            dst_ref=target,
            send_sem=self.send_sem.at[d - 1, i],
            recv_sem=self.recv_sem.at[d - 1, i],
            device_id={"tensor": lax.rem(self.me + d, self.count)},
            device_id_type=MESH,
        )

    def start(self, i, source=None):
        for d in range(1, self.count):
            self.copy(d, self.me, i, source).start()

    def arrived(self, i):
        for d in range(1, self.count):
            self.copy(d, lax.rem(self.me + self.count - d, self.count), i).wait_recv()

    def sent(self):
        @pl.loop(0, self.tiles)
        def _(i):
            for d in range(1, self.count):
                self.copy(d, self.me, i).wait_send()


def kernel(
    sizes,
    trunk, skip_mid, skip_fine,
    coarse_mid, lateral_mid, mixing_mid, coarse_fine, lateral_fine, mixing_fine, head,
    gain_mid, shift_mid, depth_mid, gain_fine, shift_fine, depth_fine,
    out,
    trunk_all, skip_mid_all, skip_fine_all, taps_mid_all, hidden_mid_all, taps_fine_all, own_all,
    partner_all,
    active_mid, active_fine,
    w_coarse_mid, w_lateral_mid, w_mixing_mid, w_coarse_fine, w_lateral_fine, w_mixing_fine,
    w_head, w_flipped,
    vectors, expanded, turned, result, doubler, reverser, swapper,
    local_sem, out_sem,
    s0, r0, s1, r1, s2, r2, s3, r3, s4, r4, s5, r5, s6, r6, s7, r7,
    mirror_send, mirror_recv, edge_send, edge_recv,
):
    tensors, contexts, tile_mid, tile_fine = sizes
    me = lax.axis_index("tensor")
    slab = lax.axis_index("context")
    strand = lax.axis_index("strand")
    after = {"context": lax.rem(slab + 1, contexts)}
    before = {"context": lax.rem(slab + contexts - 1, contexts)}
    mirror = {"context": contexts - 1 - slab, "strand": 1 - strand}
    width = active_mid.shape[1]
    tracks = w_head.shape[1]
    step = 256 if width % 256 == 0 else width
    peers = (me, tensors)

    locals_ = []
    for source, target in (
        (trunk.at[0], trunk_all.at[me]),
        (skip_mid.at[0], skip_mid_all.at[me]),
        (head, w_head),
        (coarse_mid, w_coarse_mid),
        (lateral_mid, w_lateral_mid),
        (mixing_mid, w_mixing_mid),
        (skip_fine.at[0], skip_fine_all.at[me]),
        (coarse_fine, w_coarse_fine),
        (lateral_fine, w_lateral_fine),
        (mixing_fine, w_mixing_fine),
    ):
        copy = pltpu.make_async_copy(source, target, local_sem.at[len(locals_)])
        copy.start()
        locals_.append(copy)

    barrier = pltpu.get_barrier_semaphore()
    for d in range(1, tensors):
        pl.semaphore_signal(
            barrier, inc=1, device_id={"tensor": lax.rem(me + d, tensors)}, device_id_type=MESH
        )
    for target in (after, before, mirror):
        pl.semaphore_signal(barrier, inc=1, device_id=target, device_id_type=MESH)
    pl.semaphore_wait(barrier, tensors + 2)

    g_trunk = Gather(peers, trunk_all, tile_mid // 2, s0, r0)
    g_skip_mid = Gather(peers, skip_mid_all, tile_mid, s1, r1)
    g_skip_fine = Gather(peers, skip_fine_all, tile_fine, s2, r2)
    g_taps_mid = Gather(peers, taps_mid_all, tile_mid, s3, r3)
    g_hidden_mid = Gather(peers, hidden_mid_all, tile_mid, s4, r4)
    g_taps_fine = Gather(peers, taps_fine_all, tile_fine, s5, r5)
    g_own = Gather(peers, own_all, tile_fine, s6, r6)
    g_partner = Gather(peers, partner_all, tile_fine, s7, r7)
    fine_tiles = g_own.tiles

    for k in range(g_trunk.tiles):
        g_trunk.start(k, trunk)
        g_skip_mid.start(k, skip_mid)
    first_cut, cut = max(1, fine_tiles // 4), max(1, fine_tiles // 2)
    for k in range(first_cut):
        g_skip_fine.start(k, skip_fine)
    for k, vector in enumerate((gain_mid, shift_mid, gain_fine, shift_fine)):
        vectors[k : k + 1] = vector[...].reshape(1, width)

    def iotas(shape):
        return (
            lax.broadcasted_iota(jnp.int32, shape, 0),
            lax.broadcasted_iota(jnp.int32, shape, 1),
        )

    row, column = iotas(doubler.shape)
    doubler[...] = jnp.where(
        (row == 2 * column) | (row == 2 * column + 1), 1.0, 0.0
    ).astype(jnp.bfloat16)
    row, column = iotas(reverser.shape)
    reverser[...] = jnp.where(row + column == tile_fine - 1, 1.0, 0.0).astype(jnp.bfloat16)
    row, column = iotas(swapper.shape)
    neighbour = jnp.where(lax.rem(column, 2) == 0, column + 1, column - 1)

    locals_[2].wait()

    @pl.loop(0, tracks // 256)
    def _(n):
        columns = pl.ds(pl.multiple_of(n * 256, 256), 256)
        first = me * tracks + n * 256
        flips = first < (tracks * tensors) // 2
        swapper[...] = jnp.where(
            row == jnp.where(flips, neighbour, column), 1.0, 0.0
        ).astype(jnp.bfloat16)
        for j in range(tensors):
            depth = pl.ds(j * width, width)
            w_flipped[depth, columns] = dot(w_head[depth, columns], swapper[...]).astype(
                jnp.bfloat16
            )

    def project(i, tile, coarse, lateral, w_coarse, w_lateral, k, active):
        half = pl.ds(pl.multiple_of(i * (tile // 2), EDGE), tile // 2)
        rows = pl.ds(pl.multiple_of(i * tile, EDGE), tile)
        for j in range(tensors):
            expanded[j, :tile] = dot(doubler[:tile, : tile // 2], coarse[j, half]).astype(
                jnp.bfloat16
            )

        @pl.loop(0, width // step)
        def _(n):
            columns = pl.ds(pl.multiple_of(n * step, 128), step)
            total = jnp.zeros((tile, step), jnp.float32)
            for j in range(tensors):
                depth = pl.ds(j * width, width)
                total += dot(expanded[j, :tile], w_coarse[depth, columns])
                total += dot(lateral[j, rows], w_lateral[depth, columns])
            value = gelu(vectors[k : k + 1, columns] * total + vectors[k + 1 : k + 2, columns])
            active[pl.ds(pl.multiple_of(EDGE + i * tile, EDGE), tile), columns] = value.astype(
                jnp.bfloat16
            )

    def edges(active, k):
        length = active.shape[0] - 2 * EDGE
        up = pltpu.make_async_remote_copy(
            src_ref=active.at[pl.ds(length, EDGE)],
            dst_ref=active.at[pl.ds(0, EDGE)],
            send_sem=edge_send.at[k],
            recv_sem=edge_recv.at[k],
            device_id=after,
            device_id_type=MESH,
        )
        down = pltpu.make_async_remote_copy(
            src_ref=active.at[pl.ds(EDGE, EDGE)],
            dst_ref=active.at[pl.ds(length + EDGE, EDGE)],
            send_sem=edge_send.at[k + 1],
            recv_sem=edge_recv.at[k + 1],
            device_id=before,
            device_id_type=MESH,
        )
        return up, down

    def depthwise(i, tile, tiles, active, taps, target):
        start = pl.multiple_of(i * tile, EDGE)

        @pl.loop(0, width // step)
        def _(n):
            columns = pl.ds(pl.multiple_of(n * step, 128), step)
            middle = active[pl.ds(pl.multiple_of(start + EDGE, EDGE), tile), columns].astype(
                jnp.float32
            )
            low = active[pl.ds(start, EDGE), columns].astype(jnp.float32)[EDGE - 1 :]
            high = active[
                pl.ds(pl.multiple_of(start + EDGE + tile, EDGE), EDGE), columns
            ].astype(jnp.float32)[:1]
            low = jnp.where((i == 0) & (slab == 0), 0.0, low)
            high = jnp.where((i == tiles - 1) & (slab == contexts - 1), 0.0, high)
            place = lax.broadcasted_iota(jnp.int32, middle.shape, 0)
            previous = jnp.where(place == 0, low, pltpu.roll(middle, 1, 0))
            following = jnp.where(place == tile - 1, high, pltpu.roll(middle, tile - 1, 0))
            tap = taps[:, columns].astype(jnp.float32)
            value = tap[0:1] * previous + tap[1:2] * middle + tap[2:3] * following
            target[me, pl.ds(start, tile), columns] = value.astype(jnp.bfloat16)

    def mix(i, tile, source, weight, target):
        rows = pl.ds(pl.multiple_of(i * tile, EDGE), tile)

        @pl.loop(0, width // step)
        def _(n):
            columns = pl.ds(pl.multiple_of(n * step, 128), step)
            total = jnp.zeros((tile, step), jnp.float32)
            for j in range(tensors):
                total += dot(source[j, rows], weight[pl.ds(j * width, width), columns])
            target[me, rows, columns] = total.astype(jnp.bfloat16)

    for k in (0, 1, 3, 4, 5):
        locals_[k].wait()

    def section(tiles, project_tile, taps_tile, active, k):
        up, down = edges(active, k)
        project_tile(0)
        down.start()
        project_tile(1)

        @pl.loop(1, tiles - 1)
        def _(i):
            project_tile(i + 1)

            @pl.when(i == tiles - 2)
            def _():
                up.start()

            taps_tile(i)

        down.wait_recv()
        taps_tile(tiles - 1)
        up.wait_recv()
        taps_tile(0)
        up.wait_send()
        down.wait_send()

    def project_mid(i):
        g_trunk.arrived(i)
        g_skip_mid.arrived(i)
        project(
            i, tile_mid, trunk_all, skip_mid_all, w_coarse_mid, w_lateral_mid, 0, active_mid
        )

    def taps_mid(i):
        depthwise(i, tile_mid, g_taps_mid.tiles, active_mid, depth_mid, taps_mid_all)
        g_taps_mid.start(i)

    section(g_taps_mid.tiles, project_mid, taps_mid, active_mid, 0)

    for k in range(first_cut, cut):
        g_skip_fine.start(k, skip_fine)

    @pl.loop(0, g_taps_mid.tiles)
    def _(n):
        i = lax.rem(n + 1, g_taps_mid.tiles)
        g_taps_mid.arrived(i)
        mix(i, tile_mid, taps_mid_all, w_mixing_mid, hidden_mid_all)
        g_hidden_mid.start(i)

    for k in range(cut, fine_tiles):
        g_skip_fine.start(k, skip_fine)

    for k in (6, 7, 8, 9):
        locals_[k].wait()

    @pl.loop(0, g_hidden_mid.tiles)
    def _(i):
        g_hidden_mid.arrived(i)

    def project_fine(i):
        g_skip_fine.arrived(i)
        project(
            i, tile_fine, hidden_mid_all, skip_fine_all, w_coarse_fine, w_lateral_fine, 2,
            active_fine,
        )

    def taps_fine(i):
        depthwise(i, tile_fine, fine_tiles, active_fine, depth_fine, taps_fine_all)
        g_taps_fine.start(i)

    section(fine_tiles, project_fine, taps_fine, active_fine, 2)

    def cross(i):
        return pltpu.make_async_remote_copy(
            src_ref=own_all.at[me, g_own.rows(i)],
            dst_ref=partner_all.at[me, g_own.rows(i)],
            send_sem=mirror_send.at[i],
            recv_sem=mirror_recv.at[i],
            device_id=mirror,
            device_id_type=MESH,
        )

    @pl.loop(0, fine_tiles)
    def _(n):
        i = lax.rem(n + 1, fine_tiles)
        g_taps_fine.arrived(i)
        mix(i, tile_fine, taps_fine_all, w_mixing_fine, own_all)
        cross(i).start()
        g_own.start(i)

    @pl.loop(0, fine_tiles)
    def _(i):
        g_own.arrived(i)

    def write(k):
        rows = g_own.rows(k)
        return pltpu.make_async_copy(result.at[rows], out.at[0, rows], out_sem.at[k])

    def predict(k):
        rows = g_own.rows(fine_tiles - 1 - k)
        g_partner.arrived(k)
        for j in range(tensors):
            turned[j] = dot(reverser[...], partner_all[j, g_own.rows(k)]).astype(jnp.bfloat16)

        @pl.loop(0, tracks // 256)
        def _(n):
            columns = pl.ds(pl.multiple_of(n * 256, 256), 256)
            a = jnp.zeros((tile_fine, 256), jnp.float32)
            b = jnp.zeros((tile_fine, 256), jnp.float32)
            for j in range(tensors):
                depth = pl.ds(j * width, width)
                a += dot(own_all[j, rows], w_head[depth, columns])
                b += dot(turned[j], w_flipped[depth, columns])
            result[rows, columns] = mean_softplus(a, b).astype(jnp.bfloat16)

        write(fine_tiles - 1 - k).start()

    @pl.loop(0, fine_tiles + 1)
    def _(n):
        k = lax.rem(n + 1, fine_tiles)

        @pl.when(n < fine_tiles)
        def _():
            cross(k).wait_recv()
            g_partner.start(k)

        @pl.when(n > 0)
        def _():
            predict(lax.rem(n, fine_tiles))

    for gather in (
        g_trunk, g_skip_mid, g_skip_fine, g_taps_mid, g_hidden_mid, g_taps_fine, g_own, g_partner
    ):
        gather.sent()

    @pl.loop(0, fine_tiles)
    def _(i):
        cross(i).wait_send()
        write(i).wait()


def solution(mesh):
    tensors, contexts = mesh.shape["tensor"], mesh.shape["context"]

    def on_device(
        trunk_rows, skip_mid, skip_fine, coarse_mid, lateral_mid, gain_mid, shift_mid, depth_mid,
        mixing_mid, coarse_fine, lateral_fine, gain_fine, shift_fine, depth_fine, mixing_fine,
        head_weight,
    ):
        _, coarse_rows, width = trunk_rows.shape
        mid_rows, fine_rows = skip_mid.shape[1], skip_fine.shape[1]
        depth, tracks = head_weight.shape
        tile_mid, tile_fine = min(128, mid_rows), min(128, fine_rows)
        mid_tiles, fine_tiles = mid_rows // tile_mid, fine_rows // tile_fine
        peers = max(tensors - 1, 1)
        bf16 = jnp.bfloat16

        def everyone(rows):
            return pltpu.VMEM((tensors, rows, width), bf16)

        square = pltpu.VMEM((depth, width), bf16)
        semaphores = []
        for tiles in (
            mid_tiles, mid_tiles, fine_tiles, mid_tiles, mid_tiles, fine_tiles, fine_tiles, fine_tiles
        ):
            semaphores += [pltpu.SemaphoreType.DMA((peers, tiles))] * 2
        anywhere = pl.BlockSpec(memory_space=pl.ANY)
        inside = pl.BlockSpec(memory_space=pltpu.VMEM)

        def body(*refs):
            kernel((tensors, contexts, tile_mid, tile_fine), *refs)

        macs = width * depth * (coarse_rows + 2 * mid_rows + mid_rows + 2 * fine_rows)
        macs += 2 * fine_rows * depth * tracks
        return pl.pallas_call(
            body,
            out_shape=jax.ShapeDtypeStruct((1, fine_rows, tracks), bf16),
            in_specs=[anywhere] * 10 + [inside] * 6,
            out_specs=anywhere,
            scratch_shapes=[
                everyone(coarse_rows),
                everyone(mid_rows),
                everyone(fine_rows),
                everyone(mid_rows),
                everyone(mid_rows),
                everyone(fine_rows),
                everyone(fine_rows),
                everyone(fine_rows),
                pltpu.VMEM((mid_rows + 2 * EDGE, width), bf16),
                pltpu.VMEM((fine_rows + 2 * EDGE, width), bf16),
                square, square, square, square, square, square,
                pltpu.VMEM((depth, tracks), bf16),
                pltpu.VMEM((depth, tracks), bf16),
                pltpu.VMEM((4, width), jnp.float32),
                everyone(tile_fine),
                everyone(tile_fine),
                pltpu.VMEM((fine_rows, tracks), bf16),
                pltpu.VMEM((tile_fine, tile_fine // 2), bf16),
                pltpu.VMEM((tile_fine, tile_fine), bf16),
                pltpu.VMEM((256, 256), bf16),
                pltpu.SemaphoreType.DMA((10,)),
                pltpu.SemaphoreType.DMA((fine_tiles,)),
                *semaphores,
                pltpu.SemaphoreType.DMA((fine_tiles,)),
                pltpu.SemaphoreType.DMA((fine_tiles,)),
                pltpu.SemaphoreType.DMA((4,)),
                pltpu.SemaphoreType.DMA((4,)),
            ],
            compiler_params=pltpu.CompilerParams(
                collective_id=0, has_side_effects=True, vmem_limit_bytes=60 * 2**20
            ),
            cost_estimate=pl.CostEstimate(
                flops=2 * macs, bytes_accessed=32 * 2**20, transcendentals=6 * 2**20
            ),
            name="upsample_and_predict",
        )(
            trunk_rows, skip_mid, skip_fine, coarse_mid, lateral_mid, mixing_mid, coarse_fine,
            lateral_fine, mixing_fine, head_weight, gain_mid, shift_mid, depth_mid,
            gain_fine, shift_fine, depth_fine,
        )

    rows = P("strand", ("group", "context"), "tensor")
    weight, vector = P(None, "tensor"), P("tensor")
    section = (weight, weight, vector, vector, weight, weight)
    return jax.shard_map(
        on_device,
        mesh=mesh,
        in_specs=(rows, rows, rows, *section, *section, weight),
        out_specs=rows,
        check_vma=False,
    )
```
